32 devices in a mesh: dp: 4 (over z), feature: 4 (over y, x), view: 2 (over core).
Axes of the slice: x: 2, y: 2, z: 4, core: 2. Of those that a mesh axis runs over, the one named last changes fastest.
Arguments:
- views: bfloat16 [2, 1024, 8192], P('view', 'dp'), may hold values from -64 to 64
- weight: bfloat16 [8192, 4096], P(None, ('feature', 'view')), may hold values from -1 to 1
Outputs:
- proj_grad: bfloat16 [2, 1024, 4096], P(None, 'dp', ('feature', 'view'))
- loss_value: float32 [], replicated
The draws below stay inside these ranges and needn't reach their ends.
All inputs are finite; a program needn't handle non-finite values.
Results may differ from the reference program's by a relative error of at most 0.0034.
Values may be sent and summed in bfloat16 or wider, within the bound.
A program may use at most 64 MiB of HBM per device.

```python
import jax
import jax.numpy as jnp
from jax import lax

WIDTH = 8192
FEATURES = 4096
BATCH = 1024


def row_scales(key):
    return 10.0 ** jax.random.uniform(key, (BATCH, 1), jnp.float32)


def draw_views(key, part):
    key = jax.random.fold_in(key, 11)
    keys = jax.random.split(key, 3)
    base = jnp.clip(jax.random.normal(keys[0], (BATCH, WIDTH), jnp.float32), -4.0, 4.0)
    noise = jnp.clip(jax.random.normal(keys[1], (BATCH, WIDTH), jnp.float32), -4.0, 4.0)
    scales = row_scales(keys[2])
    first_view = base * scales
    second_view = (0.8 * base + 0.6 * noise) * scales
    return jnp.stack([first_view, second_view]).astype(jnp.bfloat16)


def draw_weight(key, part):
    key = jax.random.fold_in(key, 23)
    keys = jax.random.split(key, 3)
    single = jnp.clip(jax.random.normal(keys[0], (WIDTH, FEATURES), jnp.float32), -4.0, 4.0)
    coeffs = jax.random.uniform(keys[2], (1, FEATURES), jnp.float32, 0.2, 0.6)
    shared = jnp.clip(jax.random.normal(keys[1], (WIDTH, 1), jnp.float32), -4.0, 4.0)
    return ((single + coeffs * shared) * WIDTH ** (-0.5)).astype(jnp.bfloat16)


def setup_inputs(seed: int = 0) -> dict:
    streams_of = jax.random.split(jax.random.key(seed), 3)
    return {
        "views": draw_views(jax.random.fold_in(streams_of[2], 71), 0),
        "weight": draw_weight(jax.random.fold_in(streams_of[2], 71), 0),
    }


eps = 1e-05
redundancy_weight = 0.0051

def standardize(projected):
    col_mean = lax.optimization_barrier(jnp.mean(projected, axis=1, keepdims=True))
    centered = projected - col_mean
    col_var = lax.optimization_barrier(jnp.mean(centered * centered, axis=1, keepdims=True))
    inv_std = lax.rsqrt(col_var + eps)
    return (centered * inv_std, inv_std)

def reference(views, weight):
    projected = jnp.stack([jnp.dot(views[0], weight, preferred_element_type=jnp.float32), jnp.dot(views[1], weight, preferred_element_type=jnp.float32)])
    standard, inv_std = standardize(projected)
    rounded = standard.astype(jnp.bfloat16)
    corr = jnp.dot(rounded[0].T, rounded[1], preferred_element_type=jnp.float32) / BATCH
    index = jnp.arange(FEATURES, dtype=jnp.int32)
    on_diag = index[:, None] == index[None, :]
    loss_value = jnp.sum(jnp.where(on_diag, (1.0 - corr) ** 2, redundancy_weight * corr * corr)) / FEATURES
    grad_corr = jnp.where(on_diag, -2.0 * (1.0 - corr), 2.0 * redundancy_weight * corr).astype(jnp.bfloat16)
    grad_first = jnp.dot(rounded[1], grad_corr.T, preferred_element_type=jnp.float32)
    grad_second = jnp.dot(rounded[0], grad_corr, preferred_element_type=jnp.float32)
    grad_std = jnp.stack([grad_first, grad_second])
    mean_grad = lax.optimization_barrier(jnp.mean(grad_std, axis=1, keepdims=True))
    mean_cross = lax.optimization_barrier(jnp.mean(grad_std * standard, axis=1, keepdims=True))
    proj_grad = (inv_std * (grad_std - mean_grad - standard * mean_cross)).astype(jnp.bfloat16)
    return (proj_grad, loss_value)
```

```python
import jax
import jax.numpy as jnp
from jax import lax
from jax.sharding import PartitionSpec as P

eps = 1e-05
redundancy_weight = 0.0051


def from_partner(block, axis, bit):
    count = lax.axis_size(axis)
    route = []
    for low in range(count):
        high = low | 1 << bit
        if high != low and high < count:
            route += [(low, high), (high, low)]
    return lax.ppermute(block, axis, route)


def plain(views, weight):
    shards = lax.axis_size("dp")
    local_rows = views.shape[1]
    batch = local_rows * shards
    total_cols = weight.shape[1] * lax.axis_size("feature") * lax.axis_size("view")
    partner = from_partner(views, "view", 0)
    first_here = lax.axis_index("view") == 0
    own = jnp.dot(views[0], weight, preferred_element_type=jnp.float32)
    other = jnp.dot(partner[0], weight, preferred_element_type=jnp.float32)
    projected = jnp.stack([jnp.where(first_here, own, other), jnp.where(first_here, other, own)])
    local_mean = jnp.mean(projected, axis=1, keepdims=True)
    spread = projected - local_mean
    local_sq = jnp.sum(spread * spread, axis=1, keepdims=True)
    stats = lax.all_gather(jnp.concatenate([local_mean, local_sq], axis=1), "dp")
    means, squares = stats[:, :, :1], stats[:, :, 1:]
    col_mean = jnp.mean(means, axis=0)
    shift = means - col_mean
    col_var = (jnp.sum(squares, axis=0) + local_rows * jnp.sum(shift * shift, axis=0)) / batch
    inv_std = lax.rsqrt(col_var + eps)
    standard = (projected - col_mean) * inv_std
    rounded = standard.astype(jnp.bfloat16)
    all_rows = lax.all_gather(rounded, "dp", axis=1, tiled=True)
    gram = lax.dot_general(
        rounded, all_rows, (((2,), (2,)), ((0,), (0,))), preferred_element_type=jnp.float32
    )
    gram = lax.psum(gram.astype(jnp.bfloat16), ("feature", "view"))
    diag = (
        jnp.sum(all_rows[0].astype(jnp.float32) * all_rows[1].astype(jnp.float32), axis=0) / batch
    )
    squares_part = jnp.sum(gram[0].astype(jnp.float32) * gram[1].astype(jnp.float32)) / (
        batch * float(batch)
    )
    diag_part = jnp.sum((1.0 - diag) ** 2 - redundancy_weight * diag * diag)
    members = lax.axis_size("feature") * lax.axis_size("view")
    grad_std = lax.dot_general(
        gram[::-1], all_rows, (((2,), (1,)), ((0,), (0,))), preferred_element_type=jnp.float32
    ) * (2.0 * redundancy_weight / batch)
    on_diag = (-2.0 * (1.0 - diag)).astype(jnp.bfloat16).astype(
        jnp.float32
    ) - 2.0 * redundancy_weight * diag
    grad_std = grad_std + rounded[::-1].astype(jnp.float32) * on_diag
    sum_grad, sum_cross = lax.psum(
        (
            jnp.sum(grad_std, axis=1, keepdims=True),
            jnp.sum(grad_std * standard, axis=1, keepdims=True),
        ),
        "dp",
    )
    loss_value = (
        lax.psum(
            redundancy_weight * squares_part / members + diag_part / shards,
            ("dp", "feature", "view"),
        )
        / total_cols
    )
    proj_grad = (inv_std * (grad_std - sum_grad / batch - standard * (sum_cross / batch))).astype(
        jnp.bfloat16
    )
    return (proj_grad, loss_value)


def solution(mesh):
    placed = (P("view", "dp", None), P(None, ("feature", "view")))
    return jax.shard_map(
        plain,
        mesh=mesh,
        in_specs=placed,
        out_specs=(P(None, "dp", ("feature", "view")), P()),
        check_vma=False,
    )
```

```python
import functools

import jax
import jax.numpy as jnp
from jax import lax
from jax.experimental import pallas as pl
from jax.experimental.pallas import tpu as pltpu
from jax.sharding import PartitionSpec as P

eps = 1e-05
redundancy_weight = 0.0051


def from_partner(block, axis, bit):
    count = lax.axis_size(axis)
    route = []
    for low in range(count):
        high = low | 1 << bit
        if high != low and high < count:
            route += [(low, high), (high, low)]
    return lax.ppermute(block, axis, route)


def plain(views, weight):
    shards = lax.axis_size("dp")
    local_rows = views.shape[1]
    batch = local_rows * shards
    total_cols = weight.shape[1] * lax.axis_size("feature") * lax.axis_size("view")
    partner = from_partner(views, "view", 0)
    first_here = lax.axis_index("view") == 0
    own = jnp.dot(views[0], weight, preferred_element_type=jnp.float32)
    other = jnp.dot(partner[0], weight, preferred_element_type=jnp.float32)
    projected = jnp.stack([jnp.where(first_here, own, other), jnp.where(first_here, other, own)])
    local_mean = jnp.mean(projected, axis=1, keepdims=True)
    spread = projected - local_mean
    local_sq = jnp.sum(spread * spread, axis=1, keepdims=True)
    stats = lax.all_gather(jnp.concatenate([local_mean, local_sq], axis=1), "dp")
    means, squares = stats[:, :, :1], stats[:, :, 1:]
    col_mean = jnp.mean(means, axis=0)
    shift = means - col_mean
    col_var = (jnp.sum(squares, axis=0) + local_rows * jnp.sum(shift * shift, axis=0)) / batch
    inv_std = lax.rsqrt(col_var + eps)
    standard = (projected - col_mean) * inv_std
    rounded = standard.astype(jnp.bfloat16)
    all_rows = lax.all_gather(rounded, "dp", axis=1, tiled=True)
    gram = lax.dot_general(
        rounded, all_rows, (((2,), (2,)), ((0,), (0,))), preferred_element_type=jnp.float32
    )
    gram = lax.psum(gram.astype(jnp.bfloat16), ("feature", "view"))
    diag = (
        jnp.sum(all_rows[0].astype(jnp.float32) * all_rows[1].astype(jnp.float32), axis=0) / batch
    )
    squares_part = jnp.sum(gram[0].astype(jnp.float32) * gram[1].astype(jnp.float32)) / (
        batch * float(batch)
    )
    diag_part = jnp.sum((1.0 - diag) ** 2 - redundancy_weight * diag * diag)
    members = lax.axis_size("feature") * lax.axis_size("view")
    grad_std = lax.dot_general(
        gram[::-1], all_rows, (((2,), (1,)), ((0,), (0,))), preferred_element_type=jnp.float32
    ) * (2.0 * redundancy_weight / batch)
    on_diag = (-2.0 * (1.0 - diag)).astype(jnp.bfloat16).astype(
        jnp.float32
    ) - 2.0 * redundancy_weight * diag
    grad_std = grad_std + rounded[::-1].astype(jnp.float32) * on_diag
    sum_grad, sum_cross = lax.psum(
        (
            jnp.sum(grad_std, axis=1, keepdims=True),
            jnp.sum(grad_std * standard, axis=1, keepdims=True),
        ),
        "dp",
    )
    loss_value = (
        lax.psum(
            redundancy_weight * squares_part / members + diag_part / shards,
            ("dp", "feature", "view"),
        )
        / total_cols
    )
    proj_grad = (inv_std * (grad_std - sum_grad / batch - standard * (sum_cross / batch))).astype(
        jnp.bfloat16
    )
    return (proj_grad, loss_value)


chunks = 8
vmem_bytes = 58 * 1024 * 1024
bf16, f32 = jnp.bfloat16, jnp.float32


def head_kernel(
    n,
    features,
    views_ref,
    w_ref,
    out_ref,
    loss_ref,
    w_all,
    x_all,
    proj,
    acc,
    inv,
    rall,
    k_send,
    k_recv,
    k_red,
    k_full,
    stat_send,
    stat_recv,
    fin_send,
    fin_recv,
    dg_send,
    dg_recv,
    d_part,
    sq_acc,
    w_sem,
    x_sem,
    xs_sem,
    xr_sem,
    st_s,
    st_r,
    z_s,
    z_r,
    a_s,
    a_r,
    b_s,
    b_r,
    f_s,
    f_r,
    g_s,
    g_r,
):
    members = 2 * features
    rows, width = x_all.shape[1:]
    cols = w_all.shape[1]
    batch = rows * n
    step = width // chunks
    part = rows // members
    d = lax.axis_index("dp")
    v = lax.axis_index("view")
    me = lax.axis_index("feature") * 2 + v
    u = 1 - v

    def mate(o):
        t = lax.rem(me + o, members)
        return t, {"feature": lax.div(t, 2), "view": lax.rem(t, 2)}

    def remote(src, dst, ssem, rsem, where):
        return pltpu.make_async_remote_copy(
            src_ref=src,
            dst_ref=dst,
            send_sem=ssem,
            recv_sem=rsem,
            device_id=where,
            device_id_type=pl.DeviceIdType.MESH,
        )

    def drain(ref, sem):
        pltpu.make_async_copy(ref, ref, sem).wait()

    def span(c):
        return pl.ds(pl.multiple_of(c * step, step), step)

    def w_copy(c):
        return pltpu.make_async_copy(w_ref.at[span(c), :], w_all.at[span(c), :], w_sem.at[c])

    def x_copy(c):
        return pltpu.make_async_copy(
            views_ref.at[0, :, span(c)], x_all.at[0, :, span(c)], x_sem.at[c]
        )

    def x_swap(c):
        return remote(
            views_ref.at[0, :, span(c)],
            x_all.at[1, :, span(c)],
            xs_sem.at[c],
            xr_sem.at[c],
            {"view": u},
        )

    barrier = pltpu.get_barrier_semaphore()
    for o in range(1, members):
        pl.semaphore_signal(
            barrier, inc=1, device_id=mate(o)[1], device_id_type=pl.DeviceIdType.MESH
        )
    for o in range(1, n):
        pl.semaphore_signal(
            barrier,
            inc=1,
            device_id={"dp": lax.rem(d + o, n)},
            device_id_type=pl.DeviceIdType.MESH,
        )
    for c in range(chunks):
        x_copy(c).start()
        w_copy(c).start()
    pl.semaphore_wait(barrier, members - 1 + n - 1)
    for c in range(chunks):
        x_swap(c).start()

    def multiply(slot, view, low, high):
        def body(c, carry):
            if slot == 0:
                x_copy(c).wait()
                w_copy(c).wait()
            else:
                x_swap(c).wait_recv()
            proj[view] += jnp.dot(
                x_all[slot, :, span(c)], w_all[span(c), :], preferred_element_type=f32
            )
            return carry

        lax.fori_loop(low, high, body, 0)

    row_of = lax.broadcasted_iota(jnp.int32, (8, cols), 0)

    def send_stats(view):
        p = proj[view]
        mean = jnp.sum(p, axis=0, keepdims=True) / rows
        spread = p - mean
        square = jnp.sum(spread * spread, axis=0, keepdims=True)
        stat_send[view] = jnp.where(row_of == 0, mean, square)
        for o in range(1, n):
            remote(
                stat_send.at[view],
                stat_recv.at[view, d],
                st_s.at[view],
                st_r.at[view],
                {"dp": lax.rem(d + o, n)},
            ).start()
        pltpu.make_async_copy(stat_send.at[view], stat_recv.at[view, d], st_r.at[view]).start()

    def z_copy(b, view, side):
        return remote(
            rall.at[b, view],
            rall.at[b, view],
            z_s.at[side, b, view],
            z_r.at[b, view],
            {"dp": jnp.clip(d + 1 - 2 * side, 0, n - 1)},
        )

    def pass_on(b, view, side):
        @pl.when((d < n - 1) if side == 0 else (d > 0))
        def _():
            z_copy(b, view, side).start()

    def standardize(view):
        drain(stat_recv.at[view], st_r.at[view])
        mean = jnp.zeros((1, cols), f32)
        for k in range(n):
            mean += stat_recv[view, k, 0:1]
        mean = mean / n
        var = jnp.zeros((1, cols), f32)
        for k in range(n):
            shift = stat_recv[view, k, 0:1] - mean
            var += stat_recv[view, k, 1:2] + rows * (shift * shift)
        scale = lax.rsqrt(var / batch + eps)
        inv[view] = jnp.broadcast_to(scale, (8, cols))
        s = (proj[view] - mean) * scale
        proj[view] = s
        rall[d, view] = s.astype(bf16)
        pass_on(d, view, 0)
        pass_on(d, view, 1)

    def gram_send(b, view):
        g = lax.dot_general(
            rall[d, view], rall[b, view], (((1,), (1,)), ((), ())), preferred_element_type=f32
        )
        k_send[b, view] = g.astype(bf16).reshape(members, part, rows)
        for o in range(1, members):
            t, where = mate(o)
            remote(
                k_send.at[b, view, t],
                k_recv.at[b, view, me],
                a_s.at[b, view],
                a_r.at[b, view],
                where,
            ).start()
        pltpu.make_async_copy(
            k_send.at[b, view, me], k_recv.at[b, view, me], a_r.at[b, view]
        ).start()

    def gram_sum(b, view):
        drain(k_recv.at[b, view], a_r.at[b, view])
        total = k_recv[b, view, 0].astype(f32)
        for k in range(1, members):
            total += k_recv[b, view, k].astype(f32)
        k_red[b, view] = total.astype(bf16)
        for o in range(1, members):
            remote(
                k_red.at[b, view],
                k_full.at[b, view, me],
                b_s.at[b, view],
                b_r.at[b, view],
                mate(o)[1],
            ).start()
        pltpu.make_async_copy(k_red.at[b, view], k_full.at[b, view, me], b_r.at[b, view]).start()

    def diagonal(b):
        cross = rall[b, 0].astype(f32) * rall[b, 1].astype(f32)
        d_part[b] = jnp.broadcast_to(jnp.sum(cross, axis=0, keepdims=True), (8, cols))

    def gram_use(b):
        for view in range(2):
            drain(k_full.at[b, view], b_r.at[b, view])
        first = k_full[b, 0].reshape(rows, rows)
        second = k_full[b, 1].reshape(rows, rows)
        acc[0] += jnp.dot(second, rall[b, 0], preferred_element_type=f32)
        acc[1] += jnp.dot(first, rall[b, 1], preferred_element_type=f32)
        sq_acc[...] += first.astype(f32) * second.astype(f32)

    proj[...] = jnp.zeros_like(proj)
    acc[...] = jnp.zeros_like(acc)
    sq_acc[...] = jnp.zeros_like(sq_acc)
    multiply(0, v, 0, chunks)
    send_stats(v)
    multiply(1, u, 0, chunks // 2)
    standardize(v)
    gram_send(d, v)
    multiply(1, u, chunks // 2, chunks)
    send_stats(u)
    standardize(u)
    gram_send(d, u)
    diagonal(d)
    gram_sum(d, v)
    gram_sum(d, u)
    gram_use(d)

    def hop(s, carry):
        before = (0, d - s, d - s >= 0)
        after = (1, d + s, d + s <= n - 1)
        for view in (v, u):
            for side, b, there in (before, after):

                @pl.when(there)
                def _():
                    z_copy(b, view, side).wait_recv()
                    pass_on(b, view, side)
                    gram_send(b, view)

        for side, b, there in (before, after):

            @pl.when(there)
            def _():
                diagonal(b)
                gram_sum(b, v)
                gram_sum(b, u)

        for side, b, there in (before, after):

            @pl.when(there)
            def _():
                gram_use(b)

        return carry

    lax.fori_loop(1, n, hop, 0)

    diag = jnp.zeros((1, cols), f32)
    for b in range(n):
        diag += d_part[b, 0:1]
    diag = diag / batch
    diag_loss = jnp.sum((1.0 - diag) ** 2 - redundancy_weight * diag * diag)
    dg_send[...] = jnp.full(dg_send.shape, diag_loss, f32)
    for o in range(1, members):
        remote(dg_send, dg_recv.at[me], g_s.at[0], g_r.at[0], mate(o)[1]).start()
    pltpu.make_async_copy(dg_send, dg_recv.at[me], g_r.at[0]).start()
    on_diag = (-2.0 * (1.0 - diag)).astype(bf16).astype(f32) - 2.0 * redundancy_weight * diag
    sums = jnp.full((8, cols), jnp.sum(sq_acc[...]) / batch, f32)
    for view in range(2):
        g = acc[view] * (2.0 * redundancy_weight / batch) + rall[d, 1 - view].astype(f32) * on_diag
        acc[view] = g
        sums = jnp.where(row_of == 2 * view, jnp.sum(g, axis=0, keepdims=True), sums)
        sums = jnp.where(
            row_of == 2 * view + 1, jnp.sum(g * proj[view], axis=0, keepdims=True), sums
        )
    fin_send[...] = sums
    for o in range(1, n):
        remote(
            fin_send, fin_recv.at[d], f_s.at[0], f_r.at[0], {"dp": lax.rem(d + o, n)}
        ).start()
    pltpu.make_async_copy(fin_send, fin_recv.at[d], f_r.at[0]).start()

    for c in range(chunks):
        x_swap(c).wait_send()
    for view in range(2):
        drain(stat_recv.at[view, pl.ds(0, n - 1)], st_s.at[view])
        for b in range(n):

            @pl.when((d < n - 1) & (b <= d))
            def _():
                z_copy(b, view, 0).wait_send()

            @pl.when((d > 0) & (b >= d))
            def _():
                z_copy(b, view, 1).wait_send()

            drain(k_send.at[b, view, pl.ds(0, members - 1)], a_s.at[b, view])
            drain(k_full.at[b, view, pl.ds(0, members - 1)], b_s.at[b, view])

    drain(fin_recv, f_r.at[0])
    drain(fin_recv.at[pl.ds(0, n - 1)], f_s.at[0])
    total = fin_recv[0]
    for k in range(1, n):
        total += fin_recv[k]
    total = total / batch
    for view in range(2):
        out_ref[view] = (
            inv[view, 0:1]
            * (
                acc[view]
                - total[2 * view : 2 * view + 1]
                - proj[view] * total[2 * view + 1 : 2 * view + 2]
            )
        ).astype(bf16)
    drain(dg_recv, g_r.at[0])
    drain(dg_recv.at[pl.ds(0, members - 1)], g_s.at[0])
    loss = redundancy_weight * total[4:5, 0:128]
    for k in range(members):
        loss += dg_recv[k, 0:1]
    loss_ref[...] = jnp.broadcast_to(loss / (cols * members), (8, 128))


def fused(views, weight):
    n = lax.axis_size("dp")
    features = lax.axis_size("feature")
    members = 2 * features
    rows, width = views.shape[1:]
    cols = weight.shape[1]
    part = rows // members
    return_shapes = (
        jax.ShapeDtypeStruct((2, rows, cols), bf16),
        jax.ShapeDtypeStruct((8, 128), f32),
    )
    dma = pltpu.SemaphoreType.DMA
    grad, loss = pl.pallas_call(
        functools.partial(head_kernel, n, features),
        out_shape=return_shapes,
        in_specs=[pl.BlockSpec(memory_space=pl.ANY)] * 2,
        out_specs=(pl.BlockSpec(memory_space=pltpu.VMEM),) * 2,
        scratch_shapes=[
            pltpu.VMEM((width, cols), bf16),
            pltpu.VMEM((2, rows, width), bf16),
            pltpu.VMEM((2, rows, cols), f32),
            pltpu.VMEM((2, rows, cols), f32),
            pltpu.VMEM((2, 8, cols), f32),
            pltpu.VMEM((n, 2, rows, cols), bf16),
            pltpu.VMEM((n, 2, members, part, rows), bf16),
            pltpu.VMEM((n, 2, members, part, rows), bf16),
            pltpu.VMEM((n, 2, part, rows), bf16),
            pltpu.VMEM((n, 2, members, part, rows), bf16),
            pltpu.VMEM((2, 8, cols), f32),
            pltpu.VMEM((2, n, 8, cols), f32),
            pltpu.VMEM((8, cols), f32),
            pltpu.VMEM((n, 8, cols), f32),
            pltpu.VMEM((8, 128), f32),
            pltpu.VMEM((members, 8, 128), f32),
            pltpu.VMEM((n, 8, cols), f32),
            pltpu.VMEM((rows, rows), f32),
            dma((chunks,)),
            dma((chunks,)),
            dma((chunks,)),
            dma((chunks,)),
            dma((2,)),
            dma((2,)),
            dma((2, n, 2)),
            dma((n, 2)),
            dma((n, 2)),
            dma((n, 2)),
            dma((n, 2)),
            dma((n, 2)),
            dma((1,)),
            dma((1,)),
            dma((1,)),
            dma((1,)),
        ],
        compiler_params=pltpu.CompilerParams(
            collective_id=0, has_side_effects=True, vmem_limit_bytes=vmem_bytes
        ),
    )(views, weight)
    return (grad, loss[0, 0])


def local(views, weight):
    n = lax.axis_size("dp")
    members = lax.axis_size("feature") * lax.axis_size("view")
    rows, width = views.shape[1:]
    cols = weight.shape[1]
    fits = (
        2 * (width * cols + 2 * rows * width + 8 * rows * cols)
        + 4 * n * rows * (cols + 4 * rows)
        < 32 * 1024 * 1024
    )
    even = rows % (16 * members) == 0 and rows % 128 == 0 and cols % 128 == 0
    even = even and width % (128 * chunks) == 0
    if lax.axis_size("view") == 2 and n > 1 and fits and even:
        return fused(views, weight)
    return plain(views, weight)


def solution(mesh):
    placed = (P("view", "dp", None), P(None, ("feature", "view")))
    return jax.shard_map(
        local,
        mesh=mesh,
        in_specs=placed,
        out_specs=(P(None, "dp", ("feature", "view")), P()),
        check_vma=False,
    )
```

```python
import functools

import jax
import jax.numpy as jnp
from jax import lax
from jax.experimental import pallas as pl
from jax.experimental.pallas import tpu as pltpu
from jax.sharding import PartitionSpec as P

eps = 1e-05
redundancy_weight = 0.0051


def from_partner(block, axis, bit):
    count = lax.axis_size(axis)
    route = []
    for low in range(count):
        high = low | 1 << bit
        if high != low and high < count:
            route += [(low, high), (high, low)]
    return lax.ppermute(block, axis, route)


def plain(views, weight):
    shards = lax.axis_size("dp")
    local_rows = views.shape[1]
    batch = local_rows * shards
    total_cols = weight.shape[1] * lax.axis_size("feature") * lax.axis_size("view")
    partner = from_partner(views, "view", 0)
    first_here = lax.axis_index("view") == 0
    own = jnp.dot(views[0], weight, preferred_element_type=jnp.float32)
    other = jnp.dot(partner[0], weight, preferred_element_type=jnp.float32)
    projected = jnp.stack([jnp.where(first_here, own, other), jnp.where(first_here, other, own)])
    local_mean = jnp.mean(projected, axis=1, keepdims=True)
    spread = projected - local_mean
    local_sq = jnp.sum(spread * spread, axis=1, keepdims=True)
    stats = lax.all_gather(jnp.concatenate([local_mean, local_sq], axis=1), "dp")
    means, squares = stats[:, :, :1], stats[:, :, 1:]
    col_mean = jnp.mean(means, axis=0)
    shift = means - col_mean
    col_var = (jnp.sum(squares, axis=0) + local_rows * jnp.sum(shift * shift, axis=0)) / batch
    inv_std = lax.rsqrt(col_var + eps)
    standard = (projected - col_mean) * inv_std
    rounded = standard.astype(jnp.bfloat16)
    all_rows = lax.all_gather(rounded, "dp", axis=1, tiled=True)
    gram = lax.dot_general(
        rounded, all_rows, (((2,), (2,)), ((0,), (0,))), preferred_element_type=jnp.float32
    )
    gram = lax.psum(gram.astype(jnp.bfloat16), ("feature", "view"))
    diag = (
        jnp.sum(all_rows[0].astype(jnp.float32) * all_rows[1].astype(jnp.float32), axis=0) / batch
    )
    squares_part = jnp.sum(gram[0].astype(jnp.float32) * gram[1].astype(jnp.float32)) / (
        batch * float(batch)
    )
    diag_part = jnp.sum((1.0 - diag) ** 2 - redundancy_weight * diag * diag)
    members = lax.axis_size("feature") * lax.axis_size("view")
    grad_std = lax.dot_general(
        gram[::-1], all_rows, (((2,), (1,)), ((0,), (0,))), preferred_element_type=jnp.float32
    ) * (2.0 * redundancy_weight / batch)
    on_diag = (-2.0 * (1.0 - diag)).astype(jnp.bfloat16).astype(
        jnp.float32
    ) - 2.0 * redundancy_weight * diag
    grad_std = grad_std + rounded[::-1].astype(jnp.float32) * on_diag
    sum_grad, sum_cross = lax.psum(
        (
            jnp.sum(grad_std, axis=1, keepdims=True),
            jnp.sum(grad_std * standard, axis=1, keepdims=True),
        ),
        "dp",
    )
    loss_value = (
        lax.psum(
            redundancy_weight * squares_part / members + diag_part / shards,
            ("dp", "feature", "view"),
        )
        / total_cols
    )
    proj_grad = (inv_std * (grad_std - sum_grad / batch - standard * (sum_cross / batch))).astype(
        jnp.bfloat16
    )
    return (proj_grad, loss_value)


chunks = 8
vmem_bytes = 58 * 1024 * 1024
bf16, f32 = jnp.bfloat16, jnp.float32


def head_kernel(
    n,
    features,
    views_ref,
    w_ref,
    out_ref,
    loss_ref,
    w_all,
    x_all,
    proj,
    acc,
    inv,
    rall,
    k_send,
    k_recv,
    k_red,
    k_full,
    h_send,
    h_recv,
    h_red,
    stat_send,
    stat_recv,
    fin_send,
    fin_recv,
    dg_send,
    dg_recv,
    d_part,
    sq_acc,
    w_sem,
    x_sem,
    xs_sem,
    xr_sem,
    st_s,
    st_r,
    z_s,
    z_r,
    a_s,
    a_r,
    b_s,
    b_r,
    h_as,
    h_ar,
    h_s,
    h_r,
    f_s,
    f_r,
    g_s,
    g_r,
):
    members = 2 * features
    rows, width = x_all.shape[1:]
    cols = w_all.shape[1]
    batch = rows * n
    step = width // chunks
    part = rows // members
    d = lax.axis_index("dp")
    v = lax.axis_index("view")
    me = lax.axis_index("feature") * 2 + v
    u = 1 - v

    def mate(o):
        t = lax.rem(me + o, members)
        return t, {"feature": lax.div(t, 2), "view": lax.rem(t, 2)}

    def remote(src, dst, ssem, rsem, where):
        return pltpu.make_async_remote_copy(
            src_ref=src,
            dst_ref=dst,
            send_sem=ssem,
            recv_sem=rsem,
            device_id=where,
            device_id_type=pl.DeviceIdType.MESH,
        )

    def drain(ref, sem):
        pltpu.make_async_copy(ref, ref, sem).wait()

    def span(c):
        return pl.ds(pl.multiple_of(c * step, step), step)

    def w_copy(c):
        return pltpu.make_async_copy(w_ref.at[span(c), :], w_all.at[span(c), :], w_sem.at[c])

    def x_copy(c):
        return pltpu.make_async_copy(
            views_ref.at[0, :, span(c)], x_all.at[0, :, span(c)], x_sem.at[c]
        )

    def x_swap(c):
        return remote(
            views_ref.at[0, :, span(c)],
            x_all.at[1, :, span(c)],
            xs_sem.at[c],
            xr_sem.at[c],
            {"view": u},
        )

    barrier = pltpu.get_barrier_semaphore()
    for o in range(1, members):
        pl.semaphore_signal(
            barrier, inc=1, device_id=mate(o)[1], device_id_type=pl.DeviceIdType.MESH
        )
    for o in range(1, n):
        pl.semaphore_signal(
            barrier,
            inc=1,
            device_id={"dp": lax.rem(d + o, n)},
            device_id_type=pl.DeviceIdType.MESH,
        )
    for c in range(chunks):
        x_copy(c).start()
        w_copy(c).start()
    pl.semaphore_wait(barrier, members - 1 + n - 1)
    for c in range(chunks):
        x_swap(c).start()

    def multiply(slot, view, low, high):
        def body(c, carry):
            if slot == 0:
                x_copy(c).wait()
                w_copy(c).wait()
            else:
                x_swap(c).wait_recv()
            proj[view] += jnp.dot(
                x_all[slot, :, span(c)], w_all[span(c), :], preferred_element_type=f32
            )
            return carry

        lax.fori_loop(low, high, body, 0)

    row_of = lax.broadcasted_iota(jnp.int32, (8, cols), 0)

    def send_stats(view):
        p = proj[view]
        mean = jnp.sum(p, axis=0, keepdims=True) / rows
        spread = p - mean
        square = jnp.sum(spread * spread, axis=0, keepdims=True)
        stat_send[view] = jnp.where(row_of == 0, mean, square)
        for o in range(1, n):
            remote(
                stat_send.at[view],
                stat_recv.at[view, d],
                st_s.at[view],
                st_r.at[view],
                {"dp": lax.rem(d + o, n)},
            ).start()
        pltpu.make_async_copy(stat_send.at[view], stat_recv.at[view, d], st_r.at[view]).start()

    def z_copy(b, view, side):
        return remote(
            rall.at[b, view],
            rall.at[b, view],
            z_s.at[side, b, view],
            z_r.at[b, view],
            {"dp": jnp.clip(d + 1 - 2 * side, 0, n - 1)},
        )

    def pass_on(b, view, side):
        @pl.when((d < n - 1) if side == 0 else (d > 0))
        def _():
            z_copy(b, view, side).start()

    def standardize(view):
        drain(stat_recv.at[view], st_r.at[view])
        mean = jnp.zeros((1, cols), f32)
        for k in range(n):
            mean += stat_recv[view, k, 0:1]
        mean = mean / n
        var = jnp.zeros((1, cols), f32)
        for k in range(n):
            shift = stat_recv[view, k, 0:1] - mean
            var += stat_recv[view, k, 1:2] + rows * (shift * shift)
        scale = lax.rsqrt(var / batch + eps)
        inv[view] = jnp.broadcast_to(scale, (8, cols))
        s = (proj[view] - mean) * scale
        proj[view] = s
        rall[d, view] = s.astype(bf16)
        pass_on(d, view, 0)
        pass_on(d, view, 1)

    def spread_gram(left, right, send, recv, ssem, rsem):
        g = lax.dot_general(left, right, (((1,), (1,)), ((), ())), preferred_element_type=f32)
        send[...] = g.astype(bf16).reshape(members, part, rows)
        for o in range(1, members):
            t, where = mate(o)
            remote(send.at[t], recv.at[me], ssem, rsem, where).start()
        pltpu.make_async_copy(send.at[me], recv.at[me], rsem).start()

    def add_up(recv, rsem):
        drain(recv, rsem)
        total = recv[0].astype(f32)
        for k in range(1, members):
            total += recv[k].astype(f32)
        return total.astype(bf16)

    def share_sum(b, view):
        for o in range(1, members):
            remote(
                k_red.at[b, view],
                k_full.at[b, view, me],
                b_s.at[b, view],
                b_r.at[b, view],
                mate(o)[1],
            ).start()
        pltpu.make_async_copy(k_red.at[b, view], k_full.at[b, view, me], b_r.at[b, view]).start()

    def gram_send(b, view):
        spread_gram(
            rall[d, view],
            rall[b, view],
            k_send.at[b, view],
            k_recv.at[b, view],
            a_s.at[b, view],
            a_r.at[b, view],
        )

    def gram_sum(b, view):
        k_red[b, view] = add_up(k_recv.at[b, view], a_r.at[b, view])
        share_sum(b, view)

    helps = (d == 1) | (d == n - 2)
    end = jnp.where(d == 1, 0, n - 1)
    far = n - 1 - end

    def help_copy(view):
        return remote(
            h_red.at[view], k_red.at[far, view], h_s.at[view], h_r.at[view], {"dp": end}
        )

    def help_send(view):
        spread_gram(
            rall[end, view],
            rall[far, view],
            h_send.at[view],
            h_recv.at[view],
            h_as.at[view],
            h_ar.at[view],
        )

    def help_sum(view):
        h_red[view] = add_up(h_recv.at[view], h_ar.at[view])
        help_copy(view).start()

    def relay(b, view):
        drain(k_red.at[b, view], h_r.at[view])
        share_sum(b, view)

    def diagonal(b):
        cross = rall[b, 0].astype(f32) * rall[b, 1].astype(f32)
        d_part[b] = jnp.broadcast_to(jnp.sum(cross, axis=0, keepdims=True), (8, cols))

    def gram_use(b):
        for view in range(2):
            drain(k_full.at[b, view], b_r.at[b, view])
        first = k_full[b, 0].reshape(rows, rows)
        second = k_full[b, 1].reshape(rows, rows)
        acc[0] += jnp.dot(second, rall[b, 0], preferred_element_type=f32)
        acc[1] += jnp.dot(first, rall[b, 1], preferred_element_type=f32)
        sq_acc[...] += first.astype(f32) * second.astype(f32)

    proj[...] = jnp.zeros_like(proj)
    acc[...] = jnp.zeros_like(acc)
    sq_acc[...] = jnp.zeros_like(sq_acc)
    multiply(0, v, 0, chunks)
    send_stats(v)
    multiply(1, u, 0, chunks // 2)
    standardize(v)
    multiply(1, u, chunks // 2, chunks)
    send_stats(u)
    gram_send(d, v)
    standardize(u)
    gram_send(d, u)
    diagonal(d)
    gram_sum(d, v)

    def hop(s, carry):
        sides = ((0, d - s, d - s >= 0), (1, d + s, d + s <= n - 1))
        earlier = ((d - s + 1, d - s + 1 >= 0), (d + s - 1, (d + s <= n) & (s > 1)))

        def arrive(view):
            for side, b, there in sides:

                @pl.when(there)
                def _():
                    z_copy(b, view, side).wait_recv()
                    pass_on(b, view, side)

                    @pl.when(s < n - 1)
                    def _():
                        gram_send(b, view)

            @pl.when(helps & (s == n - 2))
            def _():
                help_send(view)

        arrive(v)
        for b, there in earlier:

            @pl.when(there)
            def _():
                gram_sum(b, u)

        @pl.when(helps & (s == n - 1))
        def _():
            help_sum(u)

        for side, b, there in sides:

            @pl.when(there & (s == n - 1))
            def _():
                relay(b, v)
                relay(b, u)

        for b, there in earlier:

            @pl.when(there)
            def _():
                gram_use(b)

        arrive(u)
        for side, b, there in sides:

            @pl.when(there)
            def _():
                @pl.when(s < n - 1)
                def _():
                    gram_sum(b, v)

                diagonal(b)

        @pl.when(helps & (s == n - 2))
        def _():
            help_sum(v)

        return carry

    lax.fori_loop(1, n, hop, 0)
    for b in (0, n - 1):

        @pl.when(d == n - 1 - b)
        def _():
            gram_use(b)

    diag = jnp.zeros((1, cols), f32)
    for b in range(n):
        diag += d_part[b, 0:1]
    diag = diag / batch
    diag_loss = jnp.sum((1.0 - diag) ** 2 - redundancy_weight * diag * diag)
    dg_send[...] = jnp.full(dg_send.shape, diag_loss, f32)
    for o in range(1, members):
        remote(dg_send, dg_recv.at[me], g_s.at[0], g_r.at[0], mate(o)[1]).start()
    pltpu.make_async_copy(dg_send, dg_recv.at[me], g_r.at[0]).start()
    on_diag = (-2.0 * (1.0 - diag)).astype(bf16).astype(f32) - 2.0 * redundancy_weight * diag
    sums = jnp.full((8, cols), jnp.sum(sq_acc[...]) / batch, f32)
    for view in range(2):
        g = acc[view] * (2.0 * redundancy_weight / batch) + rall[d, 1 - view].astype(f32) * on_diag
        acc[view] = g
        sums = jnp.where(row_of == 2 * view, jnp.sum(g, axis=0, keepdims=True), sums)
        sums = jnp.where(
            row_of == 2 * view + 1, jnp.sum(g * proj[view], axis=0, keepdims=True), sums
        )
    fin_send[...] = sums
    for o in range(1, n):
        remote(
            fin_send, fin_recv.at[d], f_s.at[0], f_r.at[0], {"dp": lax.rem(d + o, n)}
        ).start()
    pltpu.make_async_copy(fin_send, fin_recv.at[d], f_r.at[0]).start()

    for c in range(chunks):
        x_swap(c).wait_send()
    for view in range(2):
        drain(stat_recv.at[view, pl.ds(0, n - 1)], st_s.at[view])

        @pl.when(helps)
        def _():
            drain(h_send.at[view, pl.ds(0, members - 1)], h_as.at[view])
            help_copy(view).wait_send()

        for b in range(n):

            @pl.when((d < n - 1) & (b <= d))
            def _():
                z_copy(b, view, 0).wait_send()

            @pl.when((d > 0) & (b >= d))
            def _():
                z_copy(b, view, 1).wait_send()

            @pl.when((b - d < n - 1) & (d - b < n - 1))
            def _():
                drain(k_send.at[b, view, pl.ds(0, members - 1)], a_s.at[b, view])

            drain(k_full.at[b, view, pl.ds(0, members - 1)], b_s.at[b, view])

    drain(fin_recv, f_r.at[0])
    drain(fin_recv.at[pl.ds(0, n - 1)], f_s.at[0])
    total = fin_recv[0]
    for k in range(1, n):
        total += fin_recv[k]
    total = total / batch
    for view in range(2):
        out_ref[view] = (
            inv[view, 0:1]
            * (
                acc[view]
                - total[2 * view : 2 * view + 1]
                - proj[view] * total[2 * view + 1 : 2 * view + 2]
            )
        ).astype(bf16)
    drain(dg_recv, g_r.at[0])
    drain(dg_recv.at[pl.ds(0, members - 1)], g_s.at[0])
    loss = redundancy_weight * total[4:5, 0:128]
    for k in range(members):
        loss += dg_recv[k, 0:1]
    loss_ref[...] = jnp.broadcast_to(loss / (cols * members), (8, 128))


def fused(views, weight):
    n = lax.axis_size("dp")
    features = lax.axis_size("feature")
    members = 2 * features
    rows, width = views.shape[1:]
    cols = weight.shape[1]
    part = rows // members
    return_shapes = (
        jax.ShapeDtypeStruct((2, rows, cols), bf16),
        jax.ShapeDtypeStruct((8, 128), f32),
    )
    dma = pltpu.SemaphoreType.DMA
    grad, loss = pl.pallas_call(
        functools.partial(head_kernel, n, features),
        out_shape=return_shapes,
        in_specs=[pl.BlockSpec(memory_space=pl.ANY)] * 2,
        out_specs=(pl.BlockSpec(memory_space=pltpu.VMEM),) * 2,
        scratch_shapes=[
            pltpu.VMEM((width, cols), bf16),
            pltpu.VMEM((2, rows, width), bf16),
            pltpu.VMEM((2, rows, cols), f32),
            pltpu.VMEM((2, rows, cols), f32),
            pltpu.VMEM((2, 8, cols), f32),
            pltpu.VMEM((n, 2, rows, cols), bf16),
            pltpu.VMEM((n, 2, members, part, rows), bf16),
            pltpu.VMEM((n, 2, members, part, rows), bf16),
            pltpu.VMEM((n, 2, part, rows), bf16),
            pltpu.VMEM((n, 2, members, part, rows), bf16),
            pltpu.VMEM((2, members, part, rows), bf16),
            pltpu.VMEM((2, members, part, rows), bf16),
            pltpu.VMEM((2, part, rows), bf16),
            pltpu.VMEM((2, 8, cols), f32),
            pltpu.VMEM((2, n, 8, cols), f32),
            pltpu.VMEM((8, cols), f32),
            pltpu.VMEM((n, 8, cols), f32),
            pltpu.VMEM((8, 128), f32),
            pltpu.VMEM((members, 8, 128), f32),
            pltpu.VMEM((n, 8, cols), f32),
            pltpu.VMEM((rows, rows), f32),
            dma((chunks,)),
            dma((chunks,)),
            dma((chunks,)),
            dma((chunks,)),
            dma((2,)),
            dma((2,)),
            dma((2, n, 2)),
            dma((n, 2)),
            dma((n, 2)),
            dma((n, 2)),
            dma((n, 2)),
            dma((n, 2)),
            dma((2,)),
            dma((2,)),
            dma((2,)),
            dma((2,)),
            dma((1,)),
            dma((1,)),
            dma((1,)),
            dma((1,)),
        ],
        compiler_params=pltpu.CompilerParams(
            collective_id=0, has_side_effects=True, vmem_limit_bytes=vmem_bytes
        ),
    )(views, weight)
    return (grad, loss[0, 0])


def local(views, weight):
    n = lax.axis_size("dp")
    members = lax.axis_size("feature") * lax.axis_size("view")
    rows, width = views.shape[1:]
    cols = weight.shape[1]
    fits = (
        2 * (width * cols + 2 * rows * width + 8 * rows * cols)
        + 4 * n * rows * (cols + 4 * rows)
        < 32 * 1024 * 1024
    )
    even = rows % (16 * members) == 0 and rows % 128 == 0 and cols % 128 == 0
    even = even and width % (128 * chunks) == 0
    if lax.axis_size("view") == 2 and n > 3 and fits and even:
        return fused(views, weight)
    return plain(views, weight)


def solution(mesh):
    placed = (P("view", "dp", None), P(None, ("feature", "view")))
    return jax.shard_map(
        local,
        mesh=mesh,
        in_specs=placed,
        out_specs=(P(None, "dp", ("feature", "view")), P()),
        check_vma=False,
    )
```

```python
import functools

import jax
import jax.numpy as jnp
from jax import lax
from jax.experimental import pallas as pl
from jax.experimental.pallas import tpu as pltpu
from jax.sharding import PartitionSpec as P

eps = 1e-05
redundancy_weight = 0.0051


def from_partner(block, axis, bit):
    count = lax.axis_size(axis)
    route = []
    for low in range(count):
        high = low | 1 << bit
        if high != low and high < count:
            route += [(low, high), (high, low)]
    return lax.ppermute(block, axis, route)


def plain(views, weight):
    shards = lax.axis_size("dp")
    local_rows = views.shape[1]
    batch = local_rows * shards
    total_cols = weight.shape[1] * lax.axis_size("feature") * lax.axis_size("view")
    partner = from_partner(views, "view", 0)
    first_here = lax.axis_index("view") == 0
    own = jnp.dot(views[0], weight, preferred_element_type=jnp.float32)
    other = jnp.dot(partner[0], weight, preferred_element_type=jnp.float32)
    projected = jnp.stack([jnp.where(first_here, own, other), jnp.where(first_here, other, own)])
    local_mean = jnp.mean(projected, axis=1, keepdims=True)
    spread = projected - local_mean
    local_sq = jnp.sum(spread * spread, axis=1, keepdims=True)
    stats = lax.all_gather(jnp.concatenate([local_mean, local_sq], axis=1), "dp")
    means, squares = stats[:, :, :1], stats[:, :, 1:]
    col_mean = jnp.mean(means, axis=0)
    shift = means - col_mean
    col_var = (jnp.sum(squares, axis=0) + local_rows * jnp.sum(shift * shift, axis=0)) / batch
    inv_std = lax.rsqrt(col_var + eps)
    standard = (projected - col_mean) * inv_std
    rounded = standard.astype(jnp.bfloat16)
    all_rows = lax.all_gather(rounded, "dp", axis=1, tiled=True)
    gram = lax.dot_general(
        rounded, all_rows, (((2,), (2,)), ((0,), (0,))), preferred_element_type=jnp.float32
    )
    gram = lax.psum(gram.astype(jnp.bfloat16), ("feature", "view"))
    diag = (
        jnp.sum(all_rows[0].astype(jnp.float32) * all_rows[1].astype(jnp.float32), axis=0) / batch
    )
    squares_part = jnp.sum(gram[0].astype(jnp.float32) * gram[1].astype(jnp.float32)) / (
        batch * float(batch)
    )
    diag_part = jnp.sum((1.0 - diag) ** 2 - redundancy_weight * diag * diag)
    members = lax.axis_size("feature") * lax.axis_size("view")
    grad_std = lax.dot_general(
        gram[::-1], all_rows, (((2,), (1,)), ((0,), (0,))), preferred_element_type=jnp.float32
    ) * (2.0 * redundancy_weight / batch)
    on_diag = (-2.0 * (1.0 - diag)).astype(jnp.bfloat16).astype(
        jnp.float32
    ) - 2.0 * redundancy_weight * diag
    grad_std = grad_std + rounded[::-1].astype(jnp.float32) * on_diag
    sum_grad, sum_cross = lax.psum(
        (
            jnp.sum(grad_std, axis=1, keepdims=True),
            jnp.sum(grad_std * standard, axis=1, keepdims=True),
        ),
        "dp",
    )
    loss_value = (
        lax.psum(
            redundancy_weight * squares_part / members + diag_part / shards,
            ("dp", "feature", "view"),
        )
        / total_cols
    )
    proj_grad = (inv_std * (grad_std - sum_grad / batch - standard * (sum_cross / batch))).astype(
        jnp.bfloat16
    )
    return (proj_grad, loss_value)


chunks = 8
vmem_bytes = 58 * 1024 * 1024
bf16, f32 = jnp.bfloat16, jnp.float32


def head_kernel(
    n,
    features,
    views_ref,
    w_ref,
    out_ref,
    loss_ref,
    w_all,
    x_all,
    proj,
    acc,
    inv,
    rall,
    k_send,
    k_recv,
    k_red,
    k_full,
    h_send,
    h_recv,
    h_red,
    stat_send,
    stat_recv,
    fin_send,
    fin_recv,
    dg_send,
    dg_recv,
    d_part,
    sq_acc,
    w_sem,
    x_sem,
    xs_sem,
    xr_sem,
    st_s,
    st_r,
    z_s,
    z_r,
    a_s,
    a_r,
    b_s,
    b_r,
    h_as,
    h_ar,
    h_s,
    h_r,
    f_s,
    f_r,
    g_s,
    g_r,
):
    members = 2 * features
    rows, width = x_all.shape[1:]
    cols = w_all.shape[1]
    batch = rows * n
    step = width // chunks
    part = rows // members
    d = lax.axis_index("dp")
    v = lax.axis_index("view")
    me = lax.axis_index("feature") * 2 + v
    u = 1 - v

    def mate(o):
        t = lax.rem(me + o, members)
        return t, {"feature": lax.div(t, 2), "view": lax.rem(t, 2)}

    def remote(src, dst, ssem, rsem, where):
        return pltpu.make_async_remote_copy(
            src_ref=src,
            dst_ref=dst,
            send_sem=ssem,
            recv_sem=rsem,
            device_id=where,
            device_id_type=pl.DeviceIdType.MESH,
        )

    def drain(ref, sem):
        pltpu.make_async_copy(ref, ref, sem).wait()

    def span(c):
        return pl.ds(pl.multiple_of(c * step, step), step)

    def w_copy(c):
        return pltpu.make_async_copy(w_ref.at[span(c), :], w_all.at[span(c), :], w_sem.at[c])

    def x_copy(c):
        return pltpu.make_async_copy(
            views_ref.at[0, :, span(c)], x_all.at[0, :, span(c)], x_sem.at[c]
        )

    def x_swap(c):
        return remote(
            views_ref.at[0, :, span(c)],
            x_all.at[1, :, span(c)],
            xs_sem.at[c],
            xr_sem.at[c],
            {"view": u},
        )

    barrier = pltpu.get_barrier_semaphore()
    for o in range(1, members):
        pl.semaphore_signal(
            barrier, inc=1, device_id=mate(o)[1], device_id_type=pl.DeviceIdType.MESH
        )
    for o in range(1, n):
        pl.semaphore_signal(
            barrier,
            inc=1,
            device_id={"dp": lax.rem(d + o, n)},
            device_id_type=pl.DeviceIdType.MESH,
        )
    for c in range(chunks):
        x_copy(c).start()
        w_copy(c).start()
    pl.semaphore_wait(barrier, members - 1 + n - 1)
    for c in range(chunks):
        x_swap(c).start()

    def multiply(slot, view, low, high):
        def body(c, carry):
            if slot == 0:
                x_copy(c).wait()
                w_copy(c).wait()
            else:
                x_swap(c).wait_recv()
            proj[view] += jnp.dot(
                x_all[slot, :, span(c)], w_all[span(c), :], preferred_element_type=f32
            )
            return carry

        lax.fori_loop(low, high, body, 0)

    row_of = lax.broadcasted_iota(jnp.int32, (8, cols), 0)

    def send_stats(view):
        p = proj[view]
        mean = jnp.sum(p, axis=0, keepdims=True) / rows
        spread = p - mean
        square = jnp.sum(spread * spread, axis=0, keepdims=True)
        stat_send[view] = jnp.where(row_of == 0, mean, square)
        for o in range(1, n):
            remote(
                stat_send.at[view],
                stat_recv.at[view, d],
                st_s.at[view],
                st_r.at[view],
                {"dp": lax.rem(d + o, n)},
            ).start()
        pltpu.make_async_copy(stat_send.at[view], stat_recv.at[view, d], st_r.at[view]).start()

    def z_copy(b, view, side):
        return remote(
            rall.at[b, view],
            rall.at[b, view],
            z_s.at[side, b, view],
            z_r.at[b, view],
            {"dp": jnp.clip(d + 1 - 2 * side, 0, n - 1)},
        )

    def pass_on(b, view, side):
        @pl.when((d < n - 1) if side == 0 else (d > 0))
        def _():
            z_copy(b, view, side).start()

    def standardize(view):
        drain(stat_recv.at[view], st_r.at[view])
        mean = jnp.zeros((1, cols), f32)
        for k in range(n):
            mean += stat_recv[view, k, 0:1]
        mean = mean / n
        var = jnp.zeros((1, cols), f32)
        for k in range(n):
            shift = stat_recv[view, k, 0:1] - mean
            var += stat_recv[view, k, 1:2] + rows * (shift * shift)
        scale = lax.rsqrt(var / batch + eps)
        inv[view] = jnp.broadcast_to(scale, (8, cols))
        s = (proj[view] - mean) * scale
        proj[view] = s
        rall[d, view] = s.astype(bf16)
        pass_on(d, view, 0)
        pass_on(d, view, 1)

    def spread_gram(left, right, send, recv, ssem, rsem):
        g = lax.dot_general(left, right, (((1,), (1,)), ((), ())), preferred_element_type=f32)
        send[...] = g.astype(bf16).reshape(members, part, rows)
        for o in range(1, members):
            t, where = mate(o)
            remote(send.at[t], recv.at[me], ssem, rsem, where).start()
        pltpu.make_async_copy(send.at[me], recv.at[me], rsem).start()

    def add_up(recv, rsem):
        drain(recv, rsem)
        total = recv[0].astype(f32)
        for k in range(1, members):
            total += recv[k].astype(f32)
        return total.astype(bf16)

    def share_sum(b, view):
        for o in range(1, members):
            remote(
                k_red.at[b, view],
                k_full.at[b, view, me],
                b_s.at[b, view],
                b_r.at[b, view],
                mate(o)[1],
            ).start()
        pltpu.make_async_copy(k_red.at[b, view], k_full.at[b, view, me], b_r.at[b, view]).start()

    def gram_send(b, view):
        spread_gram(
            rall[d, view],
            rall[b, view],
            k_send.at[b, view],
            k_recv.at[b, view],
            a_s.at[b, view],
            a_r.at[b, view],
        )

    def gram_sum(b, view):
        k_red[b, view] = add_up(k_recv.at[b, view], a_r.at[b, view])
        share_sum(b, view)

    helps = (d == 1) | (d == n - 2)
    end = jnp.where(d == 1, 0, n - 1)
    far = n - 1 - end

    def help_copy(view):
        return remote(
            h_red.at[view], k_red.at[far, view], h_s.at[view], h_r.at[view], {"dp": end}
        )

    def help_send(view):
        spread_gram(
            rall[end, view],
            rall[far, view],
            h_send.at[view],
            h_recv.at[view],
            h_as.at[view],
            h_ar.at[view],
        )

    def help_sum(view):
        h_red[view] = add_up(h_recv.at[view], h_ar.at[view])
        help_copy(view).start()

    def relay(b, view):
        drain(k_red.at[b, view], h_r.at[view])
        share_sum(b, view)

    def diagonal(b):
        cross = rall[b, 0].astype(f32) * rall[b, 1].astype(f32)
        d_part[b] = jnp.broadcast_to(jnp.sum(cross, axis=0, keepdims=True), (8, cols))

    def gram_use(b):
        for view in range(2):
            drain(k_full.at[b, view], b_r.at[b, view])
        first = k_full[b, 0].reshape(rows, rows)
        second = k_full[b, 1].reshape(rows, rows)
        acc[0] += jnp.dot(second, rall[b, 0], preferred_element_type=f32)
        acc[1] += jnp.dot(first, rall[b, 1], preferred_element_type=f32)
        sq_acc[...] += first.astype(f32) * second.astype(f32)

    proj[...] = jnp.zeros_like(proj)
    acc[...] = jnp.zeros_like(acc)
    sq_acc[...] = jnp.zeros_like(sq_acc)
    multiply(0, v, 0, chunks)
    send_stats(v)
    multiply(1, u, 0, chunks // 2)
    standardize(v)
    multiply(1, u, chunks // 2, chunks)
    send_stats(u)
    gram_send(d, v)
    standardize(u)
    gram_send(d, u)
    diagonal(d)

    def hop(s, carry):
        sides = ((0, d - s, d - s >= 0), (1, d + s, d + s <= n - 1))
        earlier = ((d - s + 1, d - s + 1 >= 0), (d + s - 1, (d + s <= n) & (s > 1)))

        def arrive(view):
            for side, b, there in sides:

                @pl.when(there)
                def _():
                    z_copy(b, view, side).wait_recv()
                    pass_on(b, view, side)

            for _, b, there in sides:

                @pl.when(there & (s < n - 1))
                def _():
                    gram_send(b, view)

            @pl.when(helps & (s == n - 2))
            def _():
                help_send(view)

        arrive(v)

        @pl.when(s == 1)
        def _():
            gram_sum(d, v)

        @pl.when(helps & (s == n - 1))
        def _():
            help_sum(u)

        for b, there in earlier:

            @pl.when(there)
            def _():
                gram_sum(b, u)

        for side, b, there in sides:

            @pl.when(there & (s == n - 1))
            def _():
                relay(b, v)
                relay(b, u)

        for b, there in earlier:

            @pl.when(there & (s == n - 1))
            def _():
                gram_use(b)

        arrive(u)
        for side, b, there in sides:

            @pl.when(there)
            def _():
                @pl.when(s < n - 1)
                def _():
                    gram_sum(b, v)

                diagonal(b)

        @pl.when(helps & (s == n - 2))
        def _():
            help_sum(v)

        for b, there in earlier:

            @pl.when(there & (s < n - 1))
            def _():
                gram_use(b)

        return carry

    lax.fori_loop(1, n, hop, 0)
    for b in (0, n - 1):

        @pl.when(d == n - 1 - b)
        def _():
            gram_use(b)

    diag = jnp.zeros((1, cols), f32)
    for b in range(n):
        diag += d_part[b, 0:1]
    diag = diag / batch
    diag_loss = jnp.sum((1.0 - diag) ** 2 - redundancy_weight * diag * diag)
    dg_send[...] = jnp.full(dg_send.shape, diag_loss, f32)
    for o in range(1, members):
        remote(dg_send, dg_recv.at[me], g_s.at[0], g_r.at[0], mate(o)[1]).start()
    pltpu.make_async_copy(dg_send, dg_recv.at[me], g_r.at[0]).start()
    on_diag = (-2.0 * (1.0 - diag)).astype(bf16).astype(f32) - 2.0 * redundancy_weight * diag
    sums = jnp.full((8, cols), jnp.sum(sq_acc[...]) / batch, f32)
    for view in range(2):
        g = acc[view] * (2.0 * redundancy_weight / batch) + rall[d, 1 - view].astype(f32) * on_diag
        acc[view] = g
        sums = jnp.where(row_of == 2 * view, jnp.sum(g, axis=0, keepdims=True), sums)
        sums = jnp.where(
            row_of == 2 * view + 1, jnp.sum(g * proj[view], axis=0, keepdims=True), sums
        )
    fin_send[...] = sums
    for o in range(1, n):
        remote(
            fin_send, fin_recv.at[d], f_s.at[0], f_r.at[0], {"dp": lax.rem(d + o, n)}
        ).start()
    pltpu.make_async_copy(fin_send, fin_recv.at[d], f_r.at[0]).start()

    for c in range(chunks):
        x_swap(c).wait_send()
    for view in range(2):
        drain(stat_recv.at[view, pl.ds(0, n - 1)], st_s.at[view])

        @pl.when(helps)
        def _():
            drain(h_send.at[view, pl.ds(0, members - 1)], h_as.at[view])
            help_copy(view).wait_send()

        for b in range(n):

            @pl.when((d < n - 1) & (b <= d))
            def _():
                z_copy(b, view, 0).wait_send()

            @pl.when((d > 0) & (b >= d))
            def _():
                z_copy(b, view, 1).wait_send()

            @pl.when((b - d < n - 1) & (d - b < n - 1))
            def _():
                drain(k_send.at[b, view, pl.ds(0, members - 1)], a_s.at[b, view])

            drain(k_full.at[b, view, pl.ds(0, members - 1)], b_s.at[b, view])

    drain(fin_recv, f_r.at[0])
    drain(fin_recv.at[pl.ds(0, n - 1)], f_s.at[0])
    total = fin_recv[0]
    for k in range(1, n):
        total += fin_recv[k]
    total = total / batch
    for view in range(2):
        out_ref[view] = (
            inv[view, 0:1]
            * (
                acc[view]
                - total[2 * view : 2 * view + 1]
                - proj[view] * total[2 * view + 1 : 2 * view + 2]
            )
        ).astype(bf16)
    drain(dg_recv, g_r.at[0])
    drain(dg_recv.at[pl.ds(0, members - 1)], g_s.at[0])
    loss = redundancy_weight * total[4:5, 0:128]
    for k in range(members):
        loss += dg_recv[k, 0:1]
    loss_ref[...] = jnp.broadcast_to(loss / (cols * members), (8, 128))


def fused(views, weight):
    n = lax.axis_size("dp")
    features = lax.axis_size("feature")
    members = 2 * features
    rows, width = views.shape[1:]
    cols = weight.shape[1]
    part = rows // members
    return_shapes = (
        jax.ShapeDtypeStruct((2, rows, cols), bf16),
        jax.ShapeDtypeStruct((8, 128), f32),
    )
    dma = pltpu.SemaphoreType.DMA
    grad, loss = pl.pallas_call(
        functools.partial(head_kernel, n, features),
        out_shape=return_shapes,
        in_specs=[pl.BlockSpec(memory_space=pl.ANY)] * 2,
        out_specs=(pl.BlockSpec(memory_space=pltpu.VMEM),) * 2,
        scratch_shapes=[
            pltpu.VMEM((width, cols), bf16),
            pltpu.VMEM((2, rows, width), bf16),
            pltpu.VMEM((2, rows, cols), f32),
            pltpu.VMEM((2, rows, cols), f32),
            pltpu.VMEM((2, 8, cols), f32),
            pltpu.VMEM((n, 2, rows, cols), bf16),
            pltpu.VMEM((n, 2, members, part, rows), bf16),
            pltpu.VMEM((n, 2, members, part, rows), bf16),
            pltpu.VMEM((n, 2, part, rows), bf16),
            pltpu.VMEM((n, 2, members, part, rows), bf16),
            pltpu.VMEM((2, members, part, rows), bf16),
            pltpu.VMEM((2, members, part, rows), bf16),
            pltpu.VMEM((2, part, rows), bf16),
            pltpu.VMEM((2, 8, cols), f32),
            pltpu.VMEM((2, n, 8, cols), f32),
            pltpu.VMEM((8, cols), f32),
            pltpu.VMEM((n, 8, cols), f32),
            pltpu.VMEM((8, 128), f32),
            pltpu.VMEM((members, 8, 128), f32),
            pltpu.VMEM((n, 8, cols), f32),
            pltpu.VMEM((rows, rows), f32),
            dma((chunks,)),
            dma((chunks,)),
            dma((chunks,)),
            dma((chunks,)),
            dma((2,)),
            dma((2,)),
            dma((2, n, 2)),
            dma((n, 2)),
            dma((n, 2)),
            dma((n, 2)),
            dma((n, 2)),
            dma((n, 2)),
            dma((2,)),
            dma((2,)),
            dma((2,)),
            dma((2,)),
            dma((1,)),
            dma((1,)),
            dma((1,)),
            dma((1,)),
        ],
        compiler_params=pltpu.CompilerParams(
            collective_id=0, has_side_effects=True, vmem_limit_bytes=vmem_bytes
        ),
    )(views, weight)
    return (grad, loss[0, 0])


def local(views, weight):
    n = lax.axis_size("dp")
    members = lax.axis_size("feature") * lax.axis_size("view")
    rows, width = views.shape[1:]
    cols = weight.shape[1]
    fits = (
        2 * (width * cols + 2 * rows * width + 8 * rows * cols)
        + 4 * n * rows * (cols + 4 * rows)
        < 32 * 1024 * 1024
    )
    even = rows % (16 * members) == 0 and rows % 128 == 0 and cols % 128 == 0
    even = even and width % (128 * chunks) == 0
    if lax.axis_size("view") == 2 and n > 3 and fits and even:
        return fused(views, weight)
    return plain(views, weight)


def solution(mesh):
    placed = (P("view", "dp", None), P(None, ("feature", "view")))
    return jax.shard_map(
        local,
        mesh=mesh,
        in_specs=placed,
        out_specs=(P(None, "dp", ("feature", "view")), P()),
        check_vma=False,
    )
```

```python
import functools

import jax
import jax.numpy as jnp
from jax import lax
from jax.experimental import pallas as pl
from jax.experimental.pallas import tpu as pltpu
from jax.sharding import PartitionSpec as P

eps = 1e-05
redundancy_weight = 0.0051


def from_partner(block, axis, bit):
    count = lax.axis_size(axis)
    route = []
    for low in range(count):
        high = low | 1 << bit
        if high != low and high < count:
            route += [(low, high), (high, low)]
    return lax.ppermute(block, axis, route)


def plain(views, weight):
    shards = lax.axis_size("dp")
    local_rows = views.shape[1]
    batch = local_rows * shards
    total_cols = weight.shape[1] * lax.axis_size("feature") * lax.axis_size("view")
    partner = from_partner(views, "view", 0)
    first_here = lax.axis_index("view") == 0
    own = jnp.dot(views[0], weight, preferred_element_type=jnp.float32)
    other = jnp.dot(partner[0], weight, preferred_element_type=jnp.float32)
    projected = jnp.stack([jnp.where(first_here, own, other), jnp.where(first_here, other, own)])
    local_mean = jnp.mean(projected, axis=1, keepdims=True)
    spread = projected - local_mean
    local_sq = jnp.sum(spread * spread, axis=1, keepdims=True)
    stats = lax.all_gather(jnp.concatenate([local_mean, local_sq], axis=1), "dp")
    means, squares = stats[:, :, :1], stats[:, :, 1:]
    col_mean = jnp.mean(means, axis=0)
    shift = means - col_mean
    col_var = (jnp.sum(squares, axis=0) + local_rows * jnp.sum(shift * shift, axis=0)) / batch
    inv_std = lax.rsqrt(col_var + eps)
    standard = (projected - col_mean) * inv_std
    rounded = standard.astype(jnp.bfloat16)
    all_rows = lax.all_gather(rounded, "dp", axis=1, tiled=True)
    gram = lax.dot_general(
        rounded, all_rows, (((2,), (2,)), ((0,), (0,))), preferred_element_type=jnp.float32
    )
    gram = lax.psum(gram.astype(jnp.bfloat16), ("feature", "view"))
    diag = (
        jnp.sum(all_rows[0].astype(jnp.float32) * all_rows[1].astype(jnp.float32), axis=0) / batch
    )
    squares_part = jnp.sum(gram[0].astype(jnp.float32) * gram[1].astype(jnp.float32)) / (
        batch * float(batch)
    )
    diag_part = jnp.sum((1.0 - diag) ** 2 - redundancy_weight * diag * diag)
    members = lax.axis_size("feature") * lax.axis_size("view")
    grad_std = lax.dot_general(
        gram[::-1], all_rows, (((2,), (1,)), ((0,), (0,))), preferred_element_type=jnp.float32
    ) * (2.0 * redundancy_weight / batch)
    on_diag = (-2.0 * (1.0 - diag)).astype(jnp.bfloat16).astype(
        jnp.float32
    ) - 2.0 * redundancy_weight * diag
    grad_std = grad_std + rounded[::-1].astype(jnp.float32) * on_diag
    sum_grad, sum_cross = lax.psum(
        (
            jnp.sum(grad_std, axis=1, keepdims=True),
            jnp.sum(grad_std * standard, axis=1, keepdims=True),
        ),
        "dp",
    )
    loss_value = (
        lax.psum(
            redundancy_weight * squares_part / members + diag_part / shards,
            ("dp", "feature", "view"),
        )
        / total_cols
    )
    proj_grad = (inv_std * (grad_std - sum_grad / batch - standard * (sum_cross / batch))).astype(
        jnp.bfloat16
    )
    return (proj_grad, loss_value)


chunks = 8
vmem_bytes = 58 * 1024 * 1024
bf16, f32 = jnp.bfloat16, jnp.float32


def head_kernel(
    n,
    features,
    views_ref,
    w_ref,
    out_ref,
    loss_ref,
    w_all,
    x_all,
    proj,
    acc,
    inv,
    rall,
    k_send,
    k_recv,
    k_red,
    k_full,
    h_send,
    h_recv,
    h_red,
    stat_send,
    stat_recv,
    fin_send,
    fin_recv,
    dg_send,
    dg_recv,
    d_part,
    sq_acc,
    w_sem,
    x_sem,
    xs_sem,
    xr_sem,
    st_s,
    st_r,
    z_s,
    z_r,
    a_s,
    a_r,
    b_s,
    b_r,
    h_as,
    h_ar,
    h_s,
    h_r,
    f_s,
    f_r,
    g_s,
    g_r,
):
    members = 2 * features
    rows, width = x_all.shape[1:]
    cols = w_all.shape[1]
    batch = rows * n
    step = width // chunks
    part = rows // members
    d = lax.axis_index("dp")
    v = lax.axis_index("view")
    me = lax.axis_index("feature") * 2 + v
    u = 1 - v

    def mate(o):
        t = lax.rem(me + o, members)
        return t, {"feature": lax.div(t, 2), "view": lax.rem(t, 2)}

    def remote(src, dst, ssem, rsem, where):
        return pltpu.make_async_remote_copy(
            src_ref=src,
            dst_ref=dst,
            send_sem=ssem,
            recv_sem=rsem,
            device_id=where,
            device_id_type=pl.DeviceIdType.MESH,
        )

    def drain(ref, sem):
        pltpu.make_async_copy(ref, ref, sem).wait()

    def span(c):
        return pl.ds(pl.multiple_of(c * step, step), step)

    def w_copy(c):
        return pltpu.make_async_copy(w_ref.at[span(c), :], w_all.at[span(c), :], w_sem.at[c])

    def x_copy(c):
        return pltpu.make_async_copy(
            views_ref.at[0, :, span(c)], x_all.at[0, :, span(c)], x_sem.at[c]
        )

    def x_swap(c):
        return remote(
            views_ref.at[0, :, span(c)],
            x_all.at[1, :, span(c)],
            xs_sem.at[c],
            xr_sem.at[c],
            {"view": u},
        )

    barrier = pltpu.get_barrier_semaphore()
    for o in range(1, members):
        pl.semaphore_signal(
            barrier, inc=1, device_id=mate(o)[1], device_id_type=pl.DeviceIdType.MESH
        )
    for o in range(1, n):
        pl.semaphore_signal(
            barrier,
            inc=1,
            device_id={"dp": lax.rem(d + o, n)},
            device_id_type=pl.DeviceIdType.MESH,
        )
    for c in range(chunks):
        x_copy(c).start()
        w_copy(c).start()
    pl.semaphore_wait(barrier, members - 1 + n - 1)
    for c in range(chunks):
        x_swap(c).start()

    def multiply(slot, view, low, high):
        def body(c, carry):
            if slot == 0:
                x_copy(c).wait()
                w_copy(c).wait()
            else:
                x_swap(c).wait_recv()
            proj[view] += jnp.dot(
                x_all[slot, :, span(c)], w_all[span(c), :], preferred_element_type=f32
            )
            return carry

        lax.fori_loop(low, high, body, 0)

    row_of = lax.broadcasted_iota(jnp.int32, (8, cols), 0)

    def send_stats(view):
        p = proj[view]
        mean = jnp.sum(p, axis=0, keepdims=True) / rows
        spread = p - mean
        square = jnp.sum(spread * spread, axis=0, keepdims=True)
        stat_send[view] = jnp.where(row_of == 0, mean, square)
        for o in range(1, n):
            remote(
                stat_send.at[view],
                stat_recv.at[view, d],
                st_s.at[view],
                st_r.at[view],
                {"dp": lax.rem(d + o, n)},
            ).start()
        pltpu.make_async_copy(stat_send.at[view], stat_recv.at[view, d], st_r.at[view]).start()

    def z_copy(b, view, side):
        return remote(
            rall.at[b, view],
            rall.at[b, view],
            z_s.at[side, b, view],
            z_r.at[b, view],
            {"dp": jnp.clip(d + 1 - 2 * side, 0, n - 1)},
        )

    def pass_on(b, view, side):
        @pl.when((d < n - 1) if side == 0 else (d > 0))
        def _():
            z_copy(b, view, side).start()

    def standardize(view):
        drain(stat_recv.at[view], st_r.at[view])
        mean = jnp.zeros((1, cols), f32)
        for k in range(n):
            mean += stat_recv[view, k, 0:1]
        mean = mean / n
        var = jnp.zeros((1, cols), f32)
        for k in range(n):
            shift = stat_recv[view, k, 0:1] - mean
            var += stat_recv[view, k, 1:2] + rows * (shift * shift)
        scale = lax.rsqrt(var / batch + eps)
        inv[view] = jnp.broadcast_to(scale, (8, cols))
        s = (proj[view] - mean) * scale
        proj[view] = s
        rall[d, view] = s.astype(bf16)
        pass_on(d, view, 0)
        pass_on(d, view, 1)

    def spread_gram(left, right, send, recv, ssem, rsem):
        g = lax.dot_general(left, right, (((1,), (1,)), ((), ())), preferred_element_type=f32)
        send[...] = g.astype(bf16).reshape(members, part, rows)
        for o in range(1, members):
            t, where = mate(o)
            remote(send.at[t], recv.at[me], ssem, rsem, where).start()
        pltpu.make_async_copy(send.at[me], recv.at[me], rsem).start()

    def add_up(recv, rsem):
        drain(recv, rsem)
        total = recv[0].astype(f32)
        for k in range(1, members):
            total += recv[k].astype(f32)
        return total.astype(bf16)

    def share_sum(b, view):
        for o in range(1, members):
            remote(
                k_red.at[b, view],
                k_full.at[b, view, me],
                b_s.at[b, view],
                b_r.at[b, view],
                mate(o)[1],
            ).start()
        pltpu.make_async_copy(k_red.at[b, view], k_full.at[b, view, me], b_r.at[b, view]).start()

    def gram_send(b, view):
        spread_gram(
            rall[d, view],
            rall[b, view],
            k_send.at[b, view],
            k_recv.at[b, view],
            a_s.at[b, view],
            a_r.at[b, view],
        )

    def gram_sum(b, view):
        k_red[b, view] = add_up(k_recv.at[b, view], a_r.at[b, view])
        share_sum(b, view)

    helps = (d == 1) | (d == n - 2)
    end = jnp.where(d == 1, 0, n - 1)
    far = n - 1 - end

    def help_copy(view):
        return remote(
            h_red.at[view], k_red.at[far, view], h_s.at[view], h_r.at[view], {"dp": end}
        )

    def help_send(view):
        spread_gram(
            rall[end, view],
            rall[far, view],
            h_send.at[view],
            h_recv.at[view],
            h_as.at[view],
            h_ar.at[view],
        )

    def help_sum(view):
        h_red[view] = add_up(h_recv.at[view], h_ar.at[view])
        help_copy(view).start()

    def relay(b, view):
        drain(k_red.at[b, view], h_r.at[view])
        share_sum(b, view)

    def diagonal(b):
        cross = rall[b, 0].astype(f32) * rall[b, 1].astype(f32)
        d_part[b] = jnp.broadcast_to(jnp.sum(cross, axis=0, keepdims=True), (8, cols))

    def gram_use(b):
        for view in range(2):
            drain(k_full.at[b, view], b_r.at[b, view])
        first = k_full[b, 0].reshape(rows, rows)
        second = k_full[b, 1].reshape(rows, rows)
        acc[0] += jnp.dot(second, rall[b, 0], preferred_element_type=f32)
        acc[1] += jnp.dot(first, rall[b, 1], preferred_element_type=f32)
        sq_acc[...] += first.astype(f32) * second.astype(f32)

    def gram_use_part(b, view):
        acc[view] += jnp.dot(
            k_full[b, 1 - view].reshape(rows, rows), rall[b, view], preferred_element_type=f32
        )

    def gram_use_early(b):
        for view in range(2):
            drain(k_full.at[b, view], b_r.at[b, view])
        gram_use_part(b, v)
        sq_acc[...] += k_full[b, 0].reshape(rows, rows).astype(f32) * k_full[b, 1].reshape(
            rows, rows
        ).astype(f32)

    proj[...] = jnp.zeros_like(proj)
    acc[...] = jnp.zeros_like(acc)
    sq_acc[...] = jnp.zeros_like(sq_acc)
    multiply(0, v, 0, chunks)
    send_stats(v)
    multiply(1, u, 0, chunks // 2)
    standardize(v)
    multiply(1, u, chunks // 2, chunks)
    send_stats(u)
    gram_send(d, v)
    standardize(u)
    gram_send(d, u)
    diagonal(d)

    def hop(s, carry):
        sides = ((0, d - s, d - s >= 0), (1, d + s, d + s <= n - 1))
        earlier = ((d - s + 1, d - s + 1 >= 0), (d + s - 1, (d + s <= n) & (s > 1)))

        def arrive(view):
            for side, b, there in sides:

                @pl.when(there)
                def _():
                    z_copy(b, view, side).wait_recv()
                    pass_on(b, view, side)

            for _, b, there in sides:

                @pl.when(there & (s < n - 1))
                def _():
                    gram_send(b, view)

            @pl.when(helps & (s == n - 2))
            def _():
                help_send(view)

        arrive(v)

        @pl.when(s == 1)
        def _():
            gram_sum(d, v)

        @pl.when(helps & (s == n - 1))
        def _():
            help_sum(u)

        for b, there in earlier:

            @pl.when(there)
            def _():
                gram_sum(b, u)

        for side, b, there in sides:

            @pl.when(there & (s == n - 1))
            def _():
                relay(b, v)
                relay(b, u)

        for b, there in earlier:

            @pl.when(there & (s == n - 1))
            def _():
                gram_use(b)

        for _, b, there in sides:

            @pl.when(there & (s == n - 1))
            def _():
                gram_use_early(b)

        arrive(u)
        for side, b, there in sides:

            @pl.when(there)
            def _():
                @pl.when(s < n - 1)
                def _():
                    gram_sum(b, v)

                diagonal(b)

        @pl.when(helps & (s == n - 2))
        def _():
            help_sum(v)

        for b, there in earlier:

            @pl.when(there & (s < n - 1))
            def _():
                gram_use(b)

        return carry

    lax.fori_loop(1, n, hop, 0)
    for b in (0, n - 1):

        @pl.when(d == n - 1 - b)
        def _():
            gram_use_part(b, u)

    diag = jnp.zeros((1, cols), f32)
    for b in range(n):
        diag += d_part[b, 0:1]
    diag = diag / batch
    diag_loss = jnp.sum((1.0 - diag) ** 2 - redundancy_weight * diag * diag)
    dg_send[...] = jnp.full(dg_send.shape, diag_loss, f32)
    for o in range(1, members):
        remote(dg_send, dg_recv.at[me], g_s.at[0], g_r.at[0], mate(o)[1]).start()
    pltpu.make_async_copy(dg_send, dg_recv.at[me], g_r.at[0]).start()
    on_diag = (-2.0 * (1.0 - diag)).astype(bf16).astype(f32) - 2.0 * redundancy_weight * diag
    sums = jnp.full((8, cols), jnp.sum(sq_acc[...]) / batch, f32)
    for view in range(2):
        g = acc[view] * (2.0 * redundancy_weight / batch) + rall[d, 1 - view].astype(f32) * on_diag
        acc[view] = g
        sums = jnp.where(row_of == 2 * view, jnp.sum(g, axis=0, keepdims=True), sums)
        sums = jnp.where(
            row_of == 2 * view + 1, jnp.sum(g * proj[view], axis=0, keepdims=True), sums
        )
    fin_send[...] = sums
    for o in range(1, n):
        remote(
            fin_send, fin_recv.at[d], f_s.at[0], f_r.at[0], {"dp": lax.rem(d + o, n)}
        ).start()
    pltpu.make_async_copy(fin_send, fin_recv.at[d], f_r.at[0]).start()

    for c in range(chunks):
        x_swap(c).wait_send()
    for view in range(2):
        drain(stat_recv.at[view, pl.ds(0, n - 1)], st_s.at[view])

        @pl.when(helps)
        def _():
            drain(h_send.at[view, pl.ds(0, members - 1)], h_as.at[view])
            help_copy(view).wait_send()

        for b in range(n):

            @pl.when((d < n - 1) & (b <= d))
            def _():
                z_copy(b, view, 0).wait_send()

            @pl.when((d > 0) & (b >= d))
            def _():
                z_copy(b, view, 1).wait_send()

            @pl.when((b - d < n - 1) & (d - b < n - 1))
            def _():
                drain(k_send.at[b, view, pl.ds(0, members - 1)], a_s.at[b, view])

            drain(k_full.at[b, view, pl.ds(0, members - 1)], b_s.at[b, view])

    drain(fin_recv, f_r.at[0])
    drain(fin_recv.at[pl.ds(0, n - 1)], f_s.at[0])
    total = fin_recv[0]
    for k in range(1, n):
        total += fin_recv[k]
    total = total / batch
    for view in range(2):
        out_ref[view] = (
            inv[view, 0:1]
            * (
                acc[view]
                - total[2 * view : 2 * view + 1]
                - proj[view] * total[2 * view + 1 : 2 * view + 2]
            )
        ).astype(bf16)
    drain(dg_recv, g_r.at[0])
    drain(dg_recv.at[pl.ds(0, members - 1)], g_s.at[0])
    loss = redundancy_weight * total[4:5, 0:128]
    for k in range(members):
        loss += dg_recv[k, 0:1]
    loss_ref[...] = jnp.broadcast_to(loss / (cols * members), (8, 128))


def fused(views, weight):
    n = lax.axis_size("dp")
    features = lax.axis_size("feature")
    members = 2 * features
    rows, width = views.shape[1:]
    cols = weight.shape[1]
    part = rows // members
    return_shapes = (
        jax.ShapeDtypeStruct((2, rows, cols), bf16),
        jax.ShapeDtypeStruct((8, 128), f32),
    )
    dma = pltpu.SemaphoreType.DMA
    grad, loss = pl.pallas_call(
        functools.partial(head_kernel, n, features),
        out_shape=return_shapes,
        in_specs=[pl.BlockSpec(memory_space=pl.ANY)] * 2,
        out_specs=(pl.BlockSpec(memory_space=pltpu.VMEM),) * 2,
        scratch_shapes=[
            pltpu.VMEM((width, cols), bf16),
            pltpu.VMEM((2, rows, width), bf16),
            pltpu.VMEM((2, rows, cols), f32),
            pltpu.VMEM((2, rows, cols), f32),
            pltpu.VMEM((2, 8, cols), f32),
            pltpu.VMEM((n, 2, rows, cols), bf16),
            pltpu.VMEM((n, 2, members, part, rows), bf16),
            pltpu.VMEM((n, 2, members, part, rows), bf16),
            pltpu.VMEM((n, 2, part, rows), bf16),
            pltpu.VMEM((n, 2, members, part, rows), bf16),
            pltpu.VMEM((2, members, part, rows), bf16),
            pltpu.VMEM((2, members, part, rows), bf16),
            pltpu.VMEM((2, part, rows), bf16),
            pltpu.VMEM((2, 8, cols), f32),
            pltpu.VMEM((2, n, 8, cols), f32),
            pltpu.VMEM((8, cols), f32),
            pltpu.VMEM((n, 8, cols), f32),
            pltpu.VMEM((8, 128), f32),
            pltpu.VMEM((members, 8, 128), f32),
            pltpu.VMEM((n, 8, cols), f32),
            pltpu.VMEM((rows, rows), f32),
            dma((chunks,)),
            dma((chunks,)),
            dma((chunks,)),
            dma((chunks,)),
            dma((2,)),
            dma((2,)),
            dma((2, n, 2)),
            dma((n, 2)),
            dma((n, 2)),
            dma((n, 2)),
            dma((n, 2)),
            dma((n, 2)),
            dma((2,)),
            dma((2,)),
            dma((2,)),
            dma((2,)),
            dma((1,)),
            dma((1,)),
            dma((1,)),
            dma((1,)),
        ],
        compiler_params=pltpu.CompilerParams(
            collective_id=0, has_side_effects=True, vmem_limit_bytes=vmem_bytes
        ),
    )(views, weight)
    return (grad, loss[0, 0])


def local(views, weight):
    n = lax.axis_size("dp")
    members = lax.axis_size("feature") * lax.axis_size("view")
    rows, width = views.shape[1:]
    cols = weight.shape[1]
    fits = (
        2 * (width * cols + 2 * rows * width + 8 * rows * cols)
        + 4 * n * rows * (cols + 4 * rows)
        < 32 * 1024 * 1024
    )
    even = rows % (16 * members) == 0 and rows % 128 == 0 and cols % 128 == 0
    even = even and width % (128 * chunks) == 0
    if lax.axis_size("view") == 2 and n > 3 and fits and even:
        return fused(views, weight)
    return plain(views, weight)


def solution(mesh):
    placed = (P("view", "dp", None), P(None, ("feature", "view")))
    return jax.shard_map(
        local,
        mesh=mesh,
        in_specs=placed,
        out_specs=(P(None, "dp", ("feature", "view")), P()),
        check_vma=False,
    )
```
